32 devices in a mesh: dom: 4 (over y, core), orb: 8 (over z, x).
Axes of the slice: x: 2, y: 2, z: 4, core: 2. Of those that a mesh axis runs over, the one named last changes fastest.
Arguments:
- psi: float32 [12288, 2048], P('dom', 'orb'), may hold values from -6 to 6
- rot: float32 [2048, 2048], P(None, 'orb'), may hold values from -0.125 to 0.125
- occ: float32 [2048], P('orb'), may hold values from 0.1 to 2
- v_loc: float32 [12288], P('dom'), may hold values from -1 to 1
Outputs:
- rotated: float32 [12288, 2048], P('dom', 'orb')
- density: float32 [12288], P('dom')
- hpsi: float32 [12288, 2048], P('dom', 'orb')
- band: float32 [2048], P('orb')
The draws below stay inside these ranges and needn't reach their ends.
All inputs are finite; a program needn't handle non-finite values.
Results may differ from the reference program's by a relative error of at most 0.000075.
Values sent between devices are 32-bit elements; how exact they have to be, the bound alone decides.
No kernel may reach another device: no remote copies, remote signals or barrier semaphores. Data moves between devices by JAX's collectives and lax.ppermute only.
A program may use at most 128 MiB of HBM per device.

```python
import math
import jax
import jax.numpy as jnp
from jax import lax

M = 2048
NY = 8
NZ = 128
NX = 12
NPTS = 12288


def levels(rng, dims, pieces, low, high):
    gain, own = 1.0, jax.random.fold_in(rng, 6)
    for dim, shards_of in pieces:
        draws = jnp.exp(jax.random.uniform(jax.random.fold_in(own, dim), (shards_of,), jnp.float32, low / len(pieces), high / len(pieces)))
        gain = gain * jnp.repeat(draws, dims[dim] // shards_of).reshape([-1 if axis == dim else 1 for axis in range(len(dims))])
    return gain


def gaussian(key, shape, deviation, reach, split=(), kind=jnp.bfloat16):
    values = jax.random.normal(key, shape, jnp.float32) * deviation
    if len(split) > 0:
        values = levels(key, shape, split, -0.22, 0.18) * values
    return jnp.clip(values, min=-reach, max=reach).astype(kind)


def setup_inputs(seed: int = 0) -> dict:
    keys = jax.random.split(jax.random.key(seed), 5)
    return {
        "psi": gaussian(keys[0], (NPTS, M), 1.0, 6.0, ((0, 4), (1, 8)), jnp.float32),
        "rot": gaussian(keys[1], (M, M), M ** -0.5, 0.125, ((1, 8),), jnp.float32),
        "occ": jnp.clip(jnp.exp(math.log(2.0) - 2.9957323 * jax.random.uniform(keys[2], (M,), jnp.float32) ** levels(keys[2], (M,), ((0, 8),), -0.2, 0.2)), 0.1, 2.0),
        "v_loc": jnp.clip(jax.random.uniform(keys[3], (NPTS,), jnp.float32, -1.0, 1.0) * levels(keys[3], (NPTS,), ((0, 4),), -0.4, 0.0), -1.0, 1.0),
    }


def reference(psi, rot, occ, v_loc):
    rotated = jnp.dot(psi, rot, precision=lax.Precision.HIGHEST, preferred_element_type=jnp.float32)
    density = jnp.sum(occ[None, :] * rotated * rotated, axis=1) / M
    potential = v_loc - (3.0 / jnp.pi) ** (1.0 / 3.0) * jnp.cbrt(density)
    field = rotated.reshape(NX, NY, NZ, M)
    beside = jnp.roll(field, 1, 0) + jnp.roll(field, -1, 0)
    beside = beside + jnp.roll(field, 1, 1) + jnp.roll(field, -1, 1)
    beside = beside + jnp.roll(field, 1, 2) + jnp.roll(field, -1, 2)
    lap = (beside - 6.0 * field).reshape(NPTS, M)
    hpsi = -0.5 * lap + potential[:, None] * rotated
    band = jnp.sum(rotated * hpsi, axis=0) / NPTS
    return rotated, density, hpsi, band
```

```python
import jax
import jax.numpy as jnp
from jax import lax
from jax.experimental import pallas as pl
from jax.experimental.pallas import tpu as pltpu
from jax.sharding import PartitionSpec as P

NY = 8
NZ = 128
EXTRA = 8


def send(block, axis, size, step):
    return lax.ppermute(block, axis, [(a, step(a)) for a in range(size)])


def halves(x):
    high = x.astype(jnp.bfloat16)
    return high, (x - high.astype(jnp.float32)).astype(jnp.bfloat16)


def split_rot(pieces, places):
    group, rows, cols = pieces[0].shape
    rows -= EXTRA
    depth = rows * len(pieces)

    def body(place, *refs):
        ins, (high, low) = refs[: len(pieces)], refs[len(pieces) :]
        for k, piece in enumerate(ins):
            at = pl.ds(pl.multiple_of(place[k] * rows, rows), rows)
            high[0, at, :], low[0, at, :] = halves(piece[0, :rows, :])

    block = pl.BlockSpec((1, rows + EXTRA, cols), lambda s, _: (s, 0, 0))
    out = pl.BlockSpec((1, depth, cols), lambda s, _: (s, 0, 0))
    shape = jax.ShapeDtypeStruct((group, depth, cols), jnp.bfloat16)
    return pl.pallas_call(
        body,
        grid_spec=pltpu.PrefetchScalarGridSpec(
            num_scalar_prefetch=1,
            grid=(group,),
            in_specs=[block] * len(pieces),
            out_specs=[out, out],
        ),
        out_shape=[shape, shape],
        compiler_params=pltpu.CompilerParams(vmem_limit_bytes=32 << 20),
        name="split_rot",
    )(places, *pieces)


def turn(blocks, sources, high, low, occ_piece, scale):
    group, depth, cols = high.shape
    rows = blocks[0].shape[0]
    count = len(blocks)
    lines = rows // NZ
    occ_row = occ_piece.shape[1] // EXTRA - 1

    def body(source, *refs):
        ins = refs[:count]
        high_ref, low_ref, occ_ref = refs[count : count + 3]
        outs = refs[count + 3 : count + 3 + group]
        x_high, x_low, dens = refs[count + 3 + group :]
        step = pl.program_id(0)

        @pl.when(step == 0)
        def _():
            for k, block in enumerate(ins):
                at = pl.ds(pl.multiple_of(source[k] * cols, cols), cols)
                x_high[:, at], x_low[:, at] = halves(block[...])

        def dot(a, b):
            return jnp.dot(a, b, preferred_element_type=jnp.float32)

        value = dot(x_low[...], high_ref[0])
        value += dot(x_high[...], low_ref[0])
        value += dot(x_high[...], high_ref[0])
        part = value * value * occ_ref[0, :1, :]
        folded = part[:, :NZ]
        for k in range(1, cols // NZ):
            folded += part[:, k * NZ : (k + 1) * NZ]

        @pl.when(step == 0)
        def _():
            dens[...] = folded

        @pl.when(step > 0)
        def _():
            dens[...] += folded

        for k, out in enumerate(outs):

            @pl.when(step == k)
            def _():
                out[:rows, :] = value

        @pl.when(step == group - 1)
        def _():
            for line in range(lines):
                sums = jnp.sum(dens[line * NZ : (line + 1) * NZ, :].T, axis=0, keepdims=True) * scale
                for out in outs:
                    out[rows + line : rows + line + 1, :NZ] = sums

    whole = pl.BlockSpec((rows, cols), lambda s, _: (0, 0))
    weight = pl.BlockSpec((1, depth, cols), lambda s, _: (s, 0, 0))
    out = pl.BlockSpec((rows + EXTRA, cols), lambda s, _: (0, 0))
    return pl.pallas_call(
        body,
        grid_spec=pltpu.PrefetchScalarGridSpec(
            num_scalar_prefetch=1,
            grid=(group,),
            in_specs=[whole] * count + [weight, weight, pl.BlockSpec((1, EXTRA, cols), lambda s, _: (s, occ_row, 0))],
            out_specs=[out] * group,
            scratch_shapes=[
                pltpu.VMEM((rows, depth), jnp.bfloat16),
                pltpu.VMEM((rows, depth), jnp.bfloat16),
                pltpu.VMEM((rows, NZ), jnp.float32),
            ],
        ),
        out_shape=[jax.ShapeDtypeStruct((rows + EXTRA, cols), jnp.float32)] * group,
        compiler_params=pltpu.CompilerParams(vmem_limit_bytes=32 << 20),
        cost_estimate=pl.CostEstimate(flops=6 * rows * depth * cols * group, bytes_accessed=4 * depth * cols * group + 8 * rows * depth, transcendentals=0),
        name="turn",
    )(sources, *blocks, high, low, occ_piece)


def finish(planes, before, after, others, v_loc, turned, group):
    cols = before.shape[-1]
    lines = NY // group
    flat = [array for plane in planes for array in plane[0]]
    kinds = [plane[1] for plane in planes]
    count = len(planes)
    points = count * NY * NZ
    factor = (3.0 / jnp.pi) ** (1.0 / 3.0)
    width = NZ

    def body(turned_ref, *refs):
        refs = list(refs)
        pieces = []
        for plane in planes:
            pieces.append([refs.pop(0) for _ in plane[0]])
        before_ref, after_ref = refs.pop(0), refs.pop(0)
        other = [[refs.pop(0) for _ in plane] for plane in others]
        v_ref, rotated, density, hpsi, band = refs
        shift = turned_ref[0]

        def tile(p, y):
            y = y % NY
            r, h = y // lines, y % lines
            if p < 0 or p == count:
                ref = before_ref if p < 0 else after_ref
                return ref[r, h * NZ : (h + 1) * NZ, :]
            if kinds[p] == "whole":
                return pieces[p][0][r, h * NZ : (h + 1) * NZ, :]
            return pieces[p][h][r, :NZ, :]

        def density_line(p, y):
            r, h = y // lines, y % lines
            if kinds[p] == "whole":
                row = other[p][0][0, r, h : h + 1, :]
                return row + other[p][0][1, r, h : h + 1, :]
            return other[p][h][0, r, :1, :] + other[p][h][1, r, :1, :]

        total = jnp.zeros((8, width), jnp.float32)
        for p in range(count):
            dens = jnp.concatenate([density_line(p, y) for y in range(NY)], axis=0)
            dens = pltpu.roll(dens, shift, 0)
            density[p * NY : (p + 1) * NY, :] = dens
            pot = v_ref[p * NY : (p + 1) * NY, :] - factor * jnp.exp(jnp.log(dens) * (1.0 / 3.0))
            pot = pltpu.roll(pot, lax.rem(NY - shift, NY), 0)
            pot = jnp.concatenate([pot, jnp.zeros((NZ - NY, NZ), jnp.float32)], axis=0).T
            for y in range(NY):
                here = tile(p, y)
                beside = tile(p - 1, y) + tile(p + 1, y) + tile(p, y - 1) + tile(p, y + 1)
                beside += pltpu.roll(here, 1, 0) + pltpu.roll(here, NZ - 1, 0)
                value = (pot[:, y : y + 1] + 3.0) * here - 0.5 * beside
                line = lax.rem(y + shift, NY)
                at = pl.ds(pl.multiple_of(p * NY * NZ + line * NZ, NZ), NZ)
                rotated[at, :] = here
                hpsi[at, :] = value
                total += jnp.sum((here * value).reshape(NZ // 8, 8, width), axis=0)
        band[...] = jnp.sum(total, axis=0, keepdims=True)

    def column(array):
        shape = array.shape
        return pl.BlockSpec(shape[:-1] + (width,), lambda c, _: (0,) * (len(shape) - 1) + (c,))

    def fixed(array):
        shape = array.shape
        return pl.BlockSpec(shape, lambda c, _: (0,) * len(shape))

    small = [array for plane in others for array in plane]
    v_lines = v_loc.reshape(count * NY, NZ)
    out_column = pl.BlockSpec((points, width), lambda c, _: (0, c))
    return pl.pallas_call(
        body,
        grid_spec=pltpu.PrefetchScalarGridSpec(
            num_scalar_prefetch=1,
            grid=(cols // width,),
            in_specs=[column(a) for a in flat] + [column(before), column(after)] + [fixed(a) for a in small] + [fixed(v_lines)],
            out_specs=[
                out_column,
                pl.BlockSpec((count * NY, NZ), lambda c, _: (0, 0)),
                out_column,
                pl.BlockSpec((1, width), lambda c, _: (0, c)),
            ],
        ),
        out_shape=[
            jax.ShapeDtypeStruct((points, cols), jnp.float32),
            jax.ShapeDtypeStruct((count * NY, NZ), jnp.float32),
            jax.ShapeDtypeStruct((points, cols), jnp.float32),
            jax.ShapeDtypeStruct((1, cols), jnp.float32),
        ],
        compiler_params=pltpu.CompilerParams(vmem_limit_bytes=40 << 20),
        name="finish",
    )(turned, *flat, before, after, *small, v_lines)


def shards(psi, rot, occ, v_loc):
    points, cols = psi.shape
    depth = rot.shape[0]
    n = lax.axis_size("orb")
    doms = lax.axis_size("dom")
    group = n // 2
    me = lax.axis_index("orb")
    dom = lax.axis_index("dom")
    pos = lax.rem(me, group)
    lines = NY // group
    plane_points = NY * NZ
    planes = points // plane_points

    rows = depth // 4
    quarter = 2 * (dom // (doms // 2)) + lax.rem(dom, 2)
    own = lax.dynamic_slice_in_dim(rot, quarter * rows, rows)
    own = jnp.concatenate([own, jnp.broadcast_to(occ[None, :], (EXTRA, cols))], axis=0)
    parts = [own]
    for s in range(1, group):
        parts.append(send(own, "orb", n, lambda a, s=s: a // group * group + (a + s) % group))
    first = jnp.stack(parts)
    second = send(first, "dom", doms, lambda a: (a + doms // 2) % doms)
    third = send(first, "dom", doms, lambda a: a ^ 1)
    fourth = send(second, "dom", doms, lambda a: a ^ 1)
    places = jnp.stack([quarter, quarter ^ 2, quarter ^ 1, quarter ^ 3]).astype(jnp.int32)
    high, low = split_rot([first, second, third, fourth], places)

    order = [0, planes - 1]
    chunks = [(p, 0, lines) for p in order]
    for p in range(1, planes - 1):
        chunks += [(p, h, 1) for h in range(lines)]
    sources = jnp.stack([lax.rem(me - s + n, n) for s in range(n)]).astype(jnp.int32)

    gathered = []
    for p, h, count in chunks:
        blocks = []
        for s in range(n):
            share = lax.rem(me + s, group)
            start = p * plane_points + (share * lines + h) * NZ
            block = lax.dynamic_slice_in_dim(psi, start, count * NZ)
            if s:
                block = send(block, "orb", n, lambda a, s=s: (a + s) % n)
            blocks.append(block)
        gathered.append(blocks)

    plane_pieces = [[] for _ in range(planes)]
    plane_others = [[] for _ in range(planes)]
    edges = {}
    for (p, h, count), blocks in zip(chunks, gathered):
        outs = turn(blocks, sources, high, low, first, 1.0 / depth)
        back = [outs[0]]
        for r in range(1, group):
            back.append(send(outs[r], "orb", n, lambda a, r=r: a // group * group + (a - r) % group))
        stack = jnp.stack(back)
        dens = stack[:, count * NZ :, :NZ]
        far = send(dens, "orb", n, lambda a: (a + group) % n)
        plane_pieces[p].append(stack)
        plane_others[p].append(jnp.stack([dens, far]))
        if p == planes - 1:
            edges["before"] = send(stack, "dom", doms, lambda a: (a + 1) % doms)
        if p == 0:
            edges["after"] = send(stack, "dom", doms, lambda a: (a - 1) % doms)

    kinds = ["whole" if p in (0, planes - 1) else "lines" for p in range(planes)]
    turned = (pos * lines).astype(jnp.int32).reshape(1)
    rotated, density, hpsi, band = finish(
        list(zip(plane_pieces, kinds)), edges["before"], edges["after"], plane_others, v_loc, turned, group
    )
    band = lax.psum(band.reshape(cols), "dom") / (points * doms)
    return rotated, density.reshape(points), hpsi, band


def solution(mesh):
    placed = (P("dom", "orb"), P(None, "orb"), P("orb"), P("dom"))
    return jax.shard_map(
        shards,
        mesh=mesh,
        in_specs=placed,
        out_specs=(P("dom", "orb"), P("dom"), P("dom", "orb"), P("orb")),
        check_vma=False,
    )
```

```python
import jax
import jax.numpy as jnp
from jax import lax
from jax.experimental import pallas as pl
from jax.experimental.pallas import tpu as pltpu
from jax.sharding import PartitionSpec as P

NY = 8
NZ = 128
EXTRA = 8
VMEM = 20 << 20
MARK = 40


def send(block, axis, size, step):
    return lax.ppermute(block, axis, [(a, step(a)) for a in range(size)])


def halves(x):
    high = x.astype(jnp.bfloat16)
    return high, (x - high.astype(jnp.float32)).astype(jnp.bfloat16)


def after(array, others):
    return lax.optimization_barrier((array, *others))[0] if others else array


def collect(pieces, span):
    rows, cols = pieces[0].shape
    count = len(pieces)

    def body(*refs):
        for k in range(count):

            @pl.when(pl.program_id(0) == k)
            def _():
                refs[-1][0] = refs[k][...]

    return pl.pallas_call(
        body,
        grid=(count,),
        in_specs=[pl.BlockSpec((rows, cols), lambda s: (0, 0))] * count,
        out_specs=pl.BlockSpec((1, rows, cols), lambda s: (s, 0, 0)),
        out_shape=jax.ShapeDtypeStruct((count, rows, cols), pieces[0].dtype),
        cost_estimate=pl.CostEstimate(flops=span * 10**9, bytes_accessed=8 * count * rows * cols, transcendentals=0),
        name="collect",
    )(*pieces)


def split_rot(sets, places):
    half, rows, cols = sets[0][0].shape
    rows -= EXTRA
    parts = len(sets[0])
    depth = rows * parts
    group = half * len(sets)

    def body(place, *refs):
        ins, (high, low, occ) = refs[: parts * len(sets)], refs[parts * len(sets) :]
        for number in range(len(sets)):

            @pl.when(pl.program_id(0) // half == number)
            def _():
                for k in range(parts):
                    piece = ins[number * parts + k]
                    at = pl.ds(pl.multiple_of(place[k] * rows, rows), rows)
                    high[0, at, :], low[0, at, :] = halves(piece[0, :rows, :])
                occ[0] = ins[number * parts][0, rows:, :]

    def block(number):
        return pl.BlockSpec((1, rows + EXTRA, cols), lambda s, _: (jnp.clip(s - number * half, 0, half - 1), 0, 0))

    def out(height):
        return pl.BlockSpec((1, height, cols), lambda s, _: (s, 0, 0))

    return pl.pallas_call(
        body,
        grid_spec=pltpu.PrefetchScalarGridSpec(
            num_scalar_prefetch=1,
            grid=(group,),
            in_specs=[block(number) for number, pieces in enumerate(sets) for _ in pieces],
            out_specs=[out(depth), out(depth), out(EXTRA)],
        ),
        out_shape=[
            jax.ShapeDtypeStruct((group, depth, cols), jnp.bfloat16),
            jax.ShapeDtypeStruct((group, depth, cols), jnp.bfloat16),
            jax.ShapeDtypeStruct((group, EXTRA, cols), jnp.float32),
        ],
        compiler_params=pltpu.CompilerParams(vmem_limit_bytes=VMEM),
        name="split_rot",
    )(places, *[piece for pieces in sets for piece in pieces])


def turn(blocks, high, low, occ, scale):
    count, rows, cols = blocks.shape
    group, depth, _ = high.shape
    lines = rows // NZ

    def body(x_ref, high_ref, low_ref, occ_ref, *refs):
        outs = refs[:group]
        dens_out, x_high, x_low, dens = refs[group:]
        step = pl.program_id(0)

        @pl.when(step == 0)
        def _():
            for k in range(count):
                at = slice(k * cols, (k + 1) * cols)
                x_high[:, at], x_low[:, at] = halves(x_ref[k])
            dens[...] = jnp.zeros_like(dens)

        def dot(a, b):
            return jnp.dot(a, b, preferred_element_type=jnp.float32)

        value = dot(x_low[...], high_ref[0])
        value += dot(x_high[...], low_ref[0])
        value += dot(x_high[...], high_ref[0])
        squares = value * value * occ_ref[0, :1, :]
        folded = squares[:, :NZ]
        for c in range(1, cols // NZ):
            folded += squares[:, c * NZ : (c + 1) * NZ]
        dens[...] += folded
        for k, out in enumerate(outs):

            @pl.when(step == k)
            def _():
                out[:rows, :] = value

        @pl.when(step == group - 1)
        def _():
            dens_out[...] = jnp.zeros_like(dens_out)
            for line in range(lines):
                sums = jnp.sum(dens[line * NZ : (line + 1) * NZ, :].T, axis=0, keepdims=True) * scale
                dens_out[line : line + 1, :] = sums
            for out in outs:
                for c in range(cols // NZ):
                    out[rows:, c * NZ : (c + 1) * NZ] = dens_out[...]

    weight = pl.BlockSpec((1, depth, cols), lambda s: (s, 0, 0))
    out = jax.ShapeDtypeStruct((rows + EXTRA, cols), jnp.float32)
    return pl.pallas_call(
        body,
        grid=(group,),
        in_specs=[pl.BlockSpec(blocks.shape, lambda s: (0, 0, 0)), weight, weight, pl.BlockSpec((1, EXTRA, cols), lambda s: (s, 0, 0))],
        out_specs=[pl.BlockSpec((rows + EXTRA, cols), lambda s: (0, 0))] * group + [pl.BlockSpec((EXTRA, NZ), lambda s: (0, 0))],
        out_shape=[out] * group + [jax.ShapeDtypeStruct((EXTRA, NZ), jnp.float32)],
        scratch_shapes=[
            pltpu.VMEM((rows, depth), jnp.bfloat16),
            pltpu.VMEM((rows, depth), jnp.bfloat16),
            pltpu.VMEM((rows, NZ), jnp.float32),
        ],
        compiler_params=pltpu.CompilerParams(vmem_limit_bytes=VMEM),
        cost_estimate=pl.CostEstimate(flops=6 * rows * depth * cols * group, bytes_accessed=4 * depth * cols * group + 8 * rows * depth, transcendentals=0),
        name="turn",
    )(blocks, high, low, occ)


def finish(planes, before, after, v_loc, places, group):
    rows, cols = before.shape[-2:]
    lines = NY // group
    count = len(planes)
    points = count * NY * NZ
    factor = (3.0 / jnp.pi) ** (1.0 / 3.0)
    width = NZ
    flat, layout, scratch = [], [], []
    for plane in planes:
        for part, shape in zip(plane, ((group, rows, width), (group, EXTRA, NZ))):
            many = isinstance(part, list)
            layout.append(len(part) if many else 0)
            flat += part if many else [part]
            if many:
                scratch.append(pltpu.VMEM(shape, jnp.float32))

    def body(place, *refs):
        refs = list(refs)
        held = refs[len(refs) - len(scratch) :]
        got = []
        for many in layout:
            if many:
                kept = held.pop(0)
                for k in range(many):
                    kept[k] = refs.pop(0)[...]
                got.append(kept)
            else:
                got.append(refs.pop(0))
        before_ref, after_ref, v_ref, rotated, density, hpsi, band = refs[:7]
        near, far = got[0::2], got[1::2]

        def tile(p, y):
            y = y % NY
            r, h = place[y // lines], y % lines
            ref = before_ref if p < 0 else after_ref if p == count else near[p]
            return ref[r, h * NZ : (h + 1) * NZ, :]

        def density_line(p, y):
            r, h = place[y // lines], y % lines
            row = rows - EXTRA + h
            return near[p][r, row : row + 1, :] + far[p][r, h : h + 1, :]

        total = jnp.zeros((8, width), jnp.float32)
        for p in range(count):
            dens = jnp.concatenate([density_line(p, y) for y in range(NY)], axis=0)
            density[p * NY : (p + 1) * NY, :] = dens
            pot = v_ref[p * NY : (p + 1) * NY, :] - factor * jnp.exp(jnp.log(dens) * (1.0 / 3.0))
            pot = jnp.concatenate([pot, jnp.zeros((NZ - NY, NZ), jnp.float32)], axis=0).T
            for y in range(NY):
                here = tile(p, y)
                beside = tile(p - 1, y) + tile(p + 1, y) + tile(p, y - 1) + tile(p, y + 1)
                beside += pltpu.roll(here, 1, 0) + pltpu.roll(here, NZ - 1, 0)
                value = (pot[:, y : y + 1] + 3.0) * here - 0.5 * beside
                at = slice((p * NY + y) * NZ, (p * NY + y + 1) * NZ)
                rotated[at, :] = here
                hpsi[at, :] = value
                total += jnp.sum((here * value).reshape(NZ // 8, 8, width), axis=0)
        band[...] = jnp.sum(total, axis=0, keepdims=True)

    def column(array):
        shape = array.shape
        if shape[-1] == cols and shape[-2] == rows:
            return pl.BlockSpec(shape[:-1] + (width,), lambda c, _: (0,) * (len(shape) - 1) + (c,))
        return pl.BlockSpec(shape, lambda c, _: (0,) * len(shape))

    v_lines = v_loc.reshape(count * NY, NZ)
    ins = [*flat, before, after, v_lines]
    out_column = pl.BlockSpec((points, width), lambda c, _: (0, c))
    return pl.pallas_call(
        body,
        grid_spec=pltpu.PrefetchScalarGridSpec(
            num_scalar_prefetch=1,
            grid=(cols // width,),
            in_specs=[column(a) for a in ins],
            out_specs=[
                out_column,
                pl.BlockSpec((count * NY, NZ), lambda c, _: (0, 0)),
                out_column,
                pl.BlockSpec((1, width), lambda c, _: (0, c)),
            ],
            scratch_shapes=scratch,
        ),
        out_shape=[
            jax.ShapeDtypeStruct((points, cols), jnp.float32),
            jax.ShapeDtypeStruct((count * NY, NZ), jnp.float32),
            jax.ShapeDtypeStruct((points, cols), jnp.float32),
            jax.ShapeDtypeStruct((1, cols), jnp.float32),
        ],
        compiler_params=pltpu.CompilerParams(vmem_limit_bytes=VMEM),
        name="finish",
    )(places, *ins)


def shards(psi, rot, occ, v_loc):
    points, cols = psi.shape
    depth = rot.shape[0]
    n = lax.axis_size("orb")
    doms = lax.axis_size("dom")
    group = n // 2
    me = lax.axis_index("orb")
    pos = lax.rem(me, group)
    dom = lax.axis_index("dom")
    plane_points = NY * NZ
    planes = points // plane_points
    shares = jnp.stack([pos ^ s for s in range(group)]).astype(jnp.int32)

    def swap(block, s):
        return send(block, "orb", n, lambda a: a ^ s)

    def across(block):
        return send(block, "dom", doms, lambda a: (a + doms // 2) % doms)

    def beside(block):
        return send(block, "dom", doms, lambda a: a ^ 1)

    rows = depth // 4
    quarter = 2 * (dom // (doms // 2)) + lax.rem(dom, 2)
    own = lax.dynamic_slice_in_dim(rot, quarter * rows, rows)
    own = jnp.concatenate([own, jnp.broadcast_to(occ[None, :], (EXTRA, cols))], axis=0)
    first = collect([own] + [swap(own, s) for s in range(1, group)], MARK)
    places = jnp.stack([quarter, quarter ^ 2, quarter ^ 1, quarter ^ 3]).astype(jnp.int32)
    second = across(first)
    third = beside(first)
    fourth = beside(second)
    high, low, occ_rows = split_rot([(first, second, third, fourth)], places)

    order = [0, planes - 1] + list(range(1, planes - 1))
    gates = [[], [first], [second, third]] + [[] for _ in order]
    done = {}
    edges = {}
    for index, p in enumerate(order):
        lot = psi[p * plane_points : (p + 1) * plane_points]
        lot = after(jnp.concatenate([lot, lot]), gates[index])
        lot = lax.all_to_all(lot, "orb", split_axis=0, concat_axis=0, tiled=True)
        gates[index + 1].append(lot)
        if index == 2:
            lot = after(lot, [done[order[1]][0]])
        *outs, dens = turn(lot.reshape(n, plane_points // group, cols), high, low, occ_rows, 1.0 / depth)
        back = [outs[0]] + [swap(outs[s], s) for s in range(1, group)]
        if index == len(order) - 1 and index > 1:
            done[p] = (back, [swap(dens, group + s) for s in range(group)])
            continue
        stack = jnp.stack(back)
        done[p] = (stack, swap(stack[:, -EXTRA:, :NZ], group))
        if p == planes - 1:
            edges["before"] = send(stack, "dom", doms, lambda a: (a + 1) % doms)
        if p == 0:
            edges["after"] = send(stack, "dom", doms, lambda a: (a - 1) % doms)

    rotated, density, hpsi, band = finish(
        [done[p] for p in range(planes)], edges["before"], edges["after"], v_loc, shares, group
    )
    band = lax.psum(band.reshape(cols), "dom") / (points * doms)
    return rotated, density.reshape(points), hpsi, band


def solution(mesh):
    placed = (P("dom", "orb"), P(None, "orb"), P("orb"), P("dom"))
    return jax.shard_map(
        shards,
        mesh=mesh,
        in_specs=placed,
        out_specs=(P("dom", "orb"), P("dom"), P("dom", "orb"), P("orb")),
        check_vma=False,
    )
```

```python
import jax
import jax.numpy as jnp
from jax import lax
from jax.experimental import pallas as pl
from jax.experimental.pallas import tpu as pltpu
from jax.sharding import PartitionSpec as P

NY = 8
NZ = 128
EXTRA = 8
VMEM = 32 << 20
MOST = 60 << 20
MARK = 40


def send(block, axis, size, step):
    return lax.ppermute(block, axis, [(a, step(a)) for a in range(size)])


def halves(x):
    high = x.astype(jnp.bfloat16)
    return high, (x - high.astype(jnp.float32)).astype(jnp.bfloat16)


def after(array, others):
    return lax.optimization_barrier((array, *others))[0] if others else array


def load(psi, parts, group):
    cols = psi.shape[1]
    heights = [rows for _, rows, _ in parts]
    total = sum(heights)

    def body(*refs):
        at = 0
        for ref, height in zip(refs, heights):
            for twice in range(2):
                refs[-1][twice, 0, at : at + height, :] = ref[...]
            at += height

    def part(first, rows, step):
        return pl.BlockSpec((rows, cols), lambda s: (first + s * step, 0))

    return pl.pallas_call(
        body,
        grid=(group,),
        in_specs=[part(*p) for p in parts],
        out_specs=pl.BlockSpec((2, 1, total, cols), lambda s: (0, s, 0, 0)),
        out_shape=jax.ShapeDtypeStruct((2, group, total, cols), psi.dtype),
        compiler_params=pltpu.CompilerParams(vmem_limit_bytes=VMEM),
        name="load",
    )(*[psi] * len(parts))


def collect(pieces, span):
    rows, cols = pieces[0].shape
    count = len(pieces)

    def body(*refs):
        for k in range(count):

            @pl.when(pl.program_id(0) == k)
            def _():
                refs[-1][0] = refs[k][...]

    return pl.pallas_call(
        body,
        grid=(count,),
        in_specs=[pl.BlockSpec((rows, cols), lambda s: (0, 0))] * count,
        out_specs=pl.BlockSpec((1, rows, cols), lambda s: (s, 0, 0)),
        out_shape=jax.ShapeDtypeStruct((count, rows, cols), pieces[0].dtype),
        cost_estimate=pl.CostEstimate(flops=span * 10**9, bytes_accessed=8 * count * rows * cols, transcendentals=0),
        name="collect",
    )(*pieces)


def split_rot(sets, places):
    _, rows, cols = sets[0][0].shape
    rows -= EXTRA
    parts = len(sets[0])
    depth = rows * parts
    sizes = [pieces[0].shape[0] for pieces in sets]
    starts = [sum(sizes[:number]) for number in range(len(sets))]
    group = sum(sizes)

    def body(place, *refs):
        ins, (high, low, occ) = refs[: parts * len(sets)], refs[parts * len(sets) :]
        step = pl.program_id(0)
        for number, (start, size) in enumerate(zip(starts, sizes)):

            @pl.when((step >= start) & (step < start + size))
            def _():
                for k in range(parts):
                    piece = ins[number * parts + k]
                    at = pl.ds(pl.multiple_of(place[k] * rows, rows), rows)
                    high[0, at, :], low[0, at, :] = halves(piece[0, :rows, :])
                occ[0] = ins[number * parts][0, rows:, :]

    def block(number):
        return pl.BlockSpec((1, rows + EXTRA, cols), lambda s, _: (jnp.clip(s - starts[number], 0, sizes[number] - 1), 0, 0))

    def out(height):
        return pl.BlockSpec((1, height, cols), lambda s, _: (s, 0, 0))

    return pl.pallas_call(
        body,
        grid_spec=pltpu.PrefetchScalarGridSpec(
            num_scalar_prefetch=1,
            grid=(group,),
            in_specs=[block(number) for number, pieces in enumerate(sets) for _ in pieces],
            out_specs=[out(depth), out(depth), out(EXTRA)],
        ),
        out_shape=[
            jax.ShapeDtypeStruct((group, depth, cols), jnp.bfloat16),
            jax.ShapeDtypeStruct((group, depth, cols), jnp.bfloat16),
            jax.ShapeDtypeStruct((group, EXTRA, cols), jnp.float32),
        ],
        compiler_params=pltpu.CompilerParams(vmem_limit_bytes=VMEM),
        name="split_rot",
    )(places, *[piece for pieces in sets for piece in pieces])


def turn(blocks, high, low, occ, scale):
    count, rows, cols = blocks.shape
    group, depth, _ = high.shape
    lines = rows // NZ

    def body(x_ref, high_ref, low_ref, occ_ref, *refs):
        outs = refs[:group]
        dens_out, x_high, x_low, dens, high_here, low_here, sems = refs[group:]
        step = pl.program_id(0)

        def copies(s):
            return (
                pltpu.make_async_copy(high_ref.at[s], high_here.at[s], sems.at[0, s]),
                pltpu.make_async_copy(low_ref.at[s], low_here.at[s], sems.at[1, s]),
            )

        @pl.when(step == 0)
        def _():
            for s in range(group):
                for copy in copies(s):
                    copy.start()
            for k in range(count):
                at = slice(k * cols, (k + 1) * cols)
                x_high[:, at], x_low[:, at] = halves(x_ref[k])
            dens[...] = jnp.zeros_like(dens)

        def dot(a, b):
            return jnp.dot(a, b, preferred_element_type=jnp.float32)

        for copy in copies(step):
            copy.wait()
        value = dot(x_low[...], high_here[step])
        value += dot(x_high[...], low_here[step])
        value += dot(x_high[...], high_here[step])
        squares = value * value * occ_ref[0, :1, :]
        folded = squares[:, :NZ]
        for c in range(1, cols // NZ):
            folded += squares[:, c * NZ : (c + 1) * NZ]
        dens[...] += folded
        for k, out in enumerate(outs):

            @pl.when(step == k)
            def _():
                out[:rows, :] = value

        @pl.when(step == group - 1)
        def _():
            dens_out[...] = jnp.zeros_like(dens_out)
            for line in range(lines):
                sums = jnp.sum(dens[line * NZ : (line + 1) * NZ, :].T, axis=0, keepdims=True) * scale
                dens_out[line : line + 1, :] = sums
            for out in outs:
                for c in range(cols // NZ):
                    out[rows:, c * NZ : (c + 1) * NZ] = dens_out[...]

    weight = pl.BlockSpec(memory_space=pltpu.HBM)
    out = jax.ShapeDtypeStruct((rows + EXTRA, cols), jnp.float32)
    return pl.pallas_call(
        body,
        grid=(group,),
        in_specs=[pl.BlockSpec(blocks.shape, lambda s: (0, 0, 0)), weight, weight, pl.BlockSpec((1, EXTRA, cols), lambda s: (s, 0, 0))],
        out_specs=[pl.BlockSpec((rows + EXTRA, cols), lambda s: (0, 0))] * group + [pl.BlockSpec((EXTRA, NZ), lambda s: (0, 0))],
        out_shape=[out] * group + [jax.ShapeDtypeStruct((EXTRA, NZ), jnp.float32)],
        scratch_shapes=[
            pltpu.VMEM((rows, depth), jnp.bfloat16),
            pltpu.VMEM((rows, depth), jnp.bfloat16),
            pltpu.VMEM((rows, NZ), jnp.float32),
            pltpu.VMEM((group, depth, cols), jnp.bfloat16),
            pltpu.VMEM((group, depth, cols), jnp.bfloat16),
            pltpu.SemaphoreType.DMA((2, group)),
        ],
        compiler_params=pltpu.CompilerParams(vmem_limit_bytes=MOST),
        cost_estimate=pl.CostEstimate(flops=6 * rows * depth * cols * group, bytes_accessed=4 * depth * cols * group + 8 * rows * depth, transcendentals=0),
        name="turn",
    )(blocks, high, low, occ)


def finish(near, far, where, before, after, v_loc, places, scale):
    cols = before.shape[-1]
    lines = len(where[0])
    count = len(where)
    points = count * NY * NZ
    factor = (3.0 / jnp.pi) ** (1.0 / 3.0)
    width = NZ
    chunks = len(near)

    def body(place, *refs):
        near_refs, far_refs = refs[:chunks], refs[chunks : 2 * chunks]
        before_ref, after_ref, v_ref, rotated, density, hpsi, band = refs[2 * chunks :]

        def tile(p, y):
            r, h = place[y % NY // lines], y % lines
            if p < 0 or p == count:
                return (before_ref if p < 0 else after_ref)[r, h * NZ : (h + 1) * NZ, :]
            chunk, line = where[p][h]
            return near_refs[chunk][r, line * NZ : (line + 1) * NZ, :]

        def density_line(p, y):
            r, (chunk, line) = place[y // lines], where[p][y % lines]
            row = near[chunk].shape[1] - EXTRA + line
            return near_refs[chunk][r, row : row + 1, :] + far_refs[chunk][r, line : line + 1, :]

        total = jnp.zeros((8, width), jnp.float32)
        for p in range(count):
            dens = jnp.concatenate([density_line(p, y) for y in range(NY)], axis=0)
            density[p * NY : (p + 1) * NY, :] = dens
            pot = v_ref[p * NY : (p + 1) * NY, :] - factor * jnp.exp(jnp.log(dens) * (1.0 / 3.0))
            pot = jnp.concatenate([pot, jnp.zeros((NZ - NY, NZ), jnp.float32)], axis=0).T
            for y in range(NY):
                here = tile(p, y)
                beside = tile(p - 1, y) + tile(p + 1, y) + tile(p, y - 1) + tile(p, y + 1)
                beside += pltpu.roll(here, 1, 0) + pltpu.roll(here, NZ - 1, 0)
                value = (pot[:, y : y + 1] + 3.0) * here - 0.5 * beside
                at = slice((p * NY + y) * NZ, (p * NY + y + 1) * NZ)
                rotated[at, :] = here
                hpsi[at, :] = value
                total += jnp.sum((here * value).reshape(NZ // 8, 8, width), axis=0)
        band[...] = jnp.sum(total, axis=0, keepdims=True) * scale

    def column(array):
        shape = array.shape
        return pl.BlockSpec(shape[:-1] + (width,), lambda c, _: (0,) * (len(shape) - 1) + (c,))

    def fixed(array):
        shape = array.shape
        return pl.BlockSpec(shape, lambda c, _: (0,) * len(shape))

    v_lines = v_loc.reshape(count * NY, NZ)
    out_column = pl.BlockSpec((points, width), lambda c, _: (0, c))
    return pl.pallas_call(
        body,
        grid_spec=pltpu.PrefetchScalarGridSpec(
            num_scalar_prefetch=1,
            grid=(cols // width,),
            in_specs=[column(a) for a in near] + [fixed(a) for a in far] + [column(before), column(after), fixed(v_lines)],
            out_specs=[
                out_column,
                pl.BlockSpec((count * NY, NZ), lambda c, _: (0, 0)),
                out_column,
                pl.BlockSpec((1, width), lambda c, _: (0, c)),
            ],
        ),
        out_shape=[
            jax.ShapeDtypeStruct((points, cols), jnp.float32),
            jax.ShapeDtypeStruct((count * NY, NZ), jnp.float32),
            jax.ShapeDtypeStruct((points, cols), jnp.float32),
            jax.ShapeDtypeStruct((1, cols), jnp.float32),
        ],
        compiler_params=pltpu.CompilerParams(vmem_limit_bytes=MOST),
        name="finish",
    )(places, *near, *far, before, after, v_lines)


def shards(psi, rot, occ, v_loc):
    points, cols = psi.shape
    depth = rot.shape[0]
    n = lax.axis_size("orb")
    doms = lax.axis_size("dom")
    group = n // 2
    me = lax.axis_index("orb")
    pos = lax.rem(me, group)
    dom = lax.axis_index("dom")
    plane_points = NY * NZ
    planes = points // plane_points
    shares = jnp.stack([pos ^ s for s in range(group)]).astype(jnp.int32)

    def swap(block, s):
        return send(block, "orb", n, lambda a: a ^ s)

    def across(block):
        return send(block, "dom", doms, lambda a: (a + doms // 2) % doms)

    def beside(block):
        return send(block, "dom", doms, lambda a: a ^ 1)

    rows = depth // 4
    quarter = 2 * (dom // (doms // 2)) + lax.rem(dom, 2)
    own = lax.dynamic_slice_in_dim(rot, quarter * rows, rows)
    own = jnp.concatenate([own, jnp.broadcast_to(occ[None, :], (EXTRA, cols))], axis=0)
    firsts = [own[None], collect([swap(own, s) for s in range(1, group)], MARK)]
    places = jnp.stack([quarter, quarter ^ 2, quarter ^ 1, quarter ^ 3]).astype(jnp.int32)
    seconds = [across(first) for first in firsts]
    thirds = [beside(first) for first in firsts]
    fourths = [beside(second) for second in seconds]
    high, low, occ_rows = split_rot(list(zip(firsts, seconds, thirds, fourths)), places)

    lines = NY // group
    ends = [(0, 0, lines), (planes - 1, 0, lines)]
    chunks = [ends] + [[(p, 0, lines)] for p in range(1, planes - 1)]
    gates = [[], [high]] + [[] for _ in chunks]
    where = [[None] * lines for _ in range(planes)]
    near, far = [], []
    for index, chunk in enumerate(chunks):
        height = 0
        lot = []
        for p, h, count in chunk:
            for k in range(count):
                where[p][h + k] = (index, height + k)
            height += count
            lot.append(((p * NY + h) // count, count * NZ, lines // count))
        lot = load(psi, lot, group).reshape(n * height * NZ, cols)
        lot = lax.all_to_all(after(lot, gates[index]), "orb", split_axis=0, concat_axis=0, tiled=True)
        gates[index + 1].append(lot)
        if index == 1:
            lot = after(lot, near)
        *outs, dens = turn(lot.reshape(n, height * NZ, cols), high, low, occ_rows, 1.0 / depth)
        near.append(jnp.stack([outs[0]] + [swap(outs[s], s) for s in range(1, group)]))
        far.append(swap(near[-1][:, -EXTRA:, :NZ], group))
        if index == 0:
            first, last = near[0][:, : lines * NZ], near[0][:, lines * NZ : 2 * lines * NZ]
            edges = [send(last, "dom", doms, lambda a: (a + 1) % doms), send(first, "dom", doms, lambda a: (a - 1) % doms)]

    rotated, density, hpsi, band = finish(
        near, far, where, *edges, v_loc, shares, 1.0 / (points * doms)
    )
    return rotated, density.reshape(points), hpsi, lax.psum(band.reshape(cols), "dom")


def solution(mesh):
    placed = (P("dom", "orb"), P(None, "orb"), P("orb"), P("dom"))
    return jax.shard_map(
        shards,
        mesh=mesh,
        in_specs=placed,
        out_specs=(P("dom", "orb"), P("dom"), P("dom", "orb"), P("orb")),
        check_vma=False,
    )
```

```python
import jax
import jax.numpy as jnp
from jax import lax
from jax.experimental import pallas as pl
from jax.experimental.pallas import tpu as pltpu
from jax.sharding import PartitionSpec as P

NY = 8
NZ = 128
EXTRA = 8
VMEM = 32 << 20
MOST = 60 << 20
MARK = 40


def send(block, axis, size, step):
    return lax.ppermute(block, axis, [(a, step(a)) for a in range(size)])


def halves(x):
    high = x.astype(jnp.bfloat16)
    return high, (x - high.astype(jnp.float32)).astype(jnp.bfloat16)


def after(array, others):
    return lax.optimization_barrier((array, *others))[0] if others else array


def load(psi, parts, group):
    cols = psi.shape[1]
    heights = [rows for _, rows, _ in parts]
    total = sum(heights)

    def body(*refs):
        at = 0
        for ref, height in zip(refs, heights):
            for twice in range(2):
                refs[-1][twice, 0, at : at + height, :] = ref[...]
            at += height

    def part(first, rows, step):
        return pl.BlockSpec((rows, cols), lambda s: (first + s * step, 0))

    return pl.pallas_call(
        body,
        grid=(group,),
        in_specs=[part(*p) for p in parts],
        out_specs=pl.BlockSpec((2, 1, total, cols), lambda s: (0, s, 0, 0)),
        out_shape=jax.ShapeDtypeStruct((2, group, total, cols), psi.dtype),
        compiler_params=pltpu.CompilerParams(vmem_limit_bytes=VMEM),
        name="load",
    )(*[psi] * len(parts))


def collect(pieces, span):
    rows, cols = pieces[0].shape
    count = len(pieces)

    def body(*refs):
        for k in range(count):

            @pl.when(pl.program_id(0) == k)
            def _():
                refs[-1][0] = refs[k][...]

    return pl.pallas_call(
        body,
        grid=(count,),
        in_specs=[pl.BlockSpec((rows, cols), lambda s: (0, 0))] * count,
        out_specs=pl.BlockSpec((1, rows, cols), lambda s: (s, 0, 0)),
        out_shape=jax.ShapeDtypeStruct((count, rows, cols), pieces[0].dtype),
        cost_estimate=pl.CostEstimate(flops=span * 10**9, bytes_accessed=8 * count * rows * cols, transcendentals=0),
        name="collect",
    )(*pieces)


def split_rot(sets, places):
    _, rows, cols = sets[0][0].shape
    rows -= EXTRA
    parts = len(sets[0])
    depth = rows * parts
    sizes = [pieces[0].shape[0] for pieces in sets]
    starts = [sum(sizes[:number]) for number in range(len(sets))]
    group = sum(sizes)

    def body(place, *refs):
        ins, (high, low, occ) = refs[: parts * len(sets)], refs[parts * len(sets) :]
        step = pl.program_id(0)
        for number, (start, size) in enumerate(zip(starts, sizes)):

            @pl.when((step >= start) & (step < start + size))
            def _():
                for k in range(parts):
                    piece = ins[number * parts + k]
                    at = pl.ds(pl.multiple_of(place[k] * rows, rows), rows)
                    high[0, at, :], low[0, at, :] = halves(piece[0, :rows, :])
                occ[0] = ins[number * parts][0, rows:, :]

    def block(number):
        return pl.BlockSpec((1, rows + EXTRA, cols), lambda s, _: (jnp.clip(s - starts[number], 0, sizes[number] - 1), 0, 0))

    def out(height):
        return pl.BlockSpec((1, height, cols), lambda s, _: (s, 0, 0))

    return pl.pallas_call(
        body,
        grid_spec=pltpu.PrefetchScalarGridSpec(
            num_scalar_prefetch=1,
            grid=(group,),
            in_specs=[block(number) for number, pieces in enumerate(sets) for _ in pieces],
            out_specs=[out(depth), out(depth), out(EXTRA)],
        ),
        out_shape=[
            jax.ShapeDtypeStruct((group, depth, cols), jnp.bfloat16),
            jax.ShapeDtypeStruct((group, depth, cols), jnp.bfloat16),
            jax.ShapeDtypeStruct((group, EXTRA, cols), jnp.float32),
        ],
        compiler_params=pltpu.CompilerParams(vmem_limit_bytes=VMEM),
        name="split_rot",
    )(places, *[piece for pieces in sets for piece in pieces])


def turn(blocks, first, rows, high, low, occ, scale):
    count, _, cols = blocks.shape
    group, depth, _ = high.shape
    lines = rows // NZ

    def body(x_ref, high_ref, low_ref, occ_ref, *refs):
        outs = refs[:group]
        dens_out, x_high, x_low, dens, high_here, low_here, sems = refs[group:]
        step = pl.program_id(0)

        def copies(s):
            return (
                pltpu.make_async_copy(high_ref.at[s], high_here.at[s], sems.at[0, s]),
                pltpu.make_async_copy(low_ref.at[s], low_here.at[s], sems.at[1, s]),
            )

        @pl.when(step == 0)
        def _():
            for s in range(group):
                for copy in copies(s):
                    copy.start()
            for k in range(count):
                at = slice(k * cols, (k + 1) * cols)
                x_high[:, at], x_low[:, at] = halves(x_ref[k])
            dens[...] = jnp.zeros_like(dens)

        def dot(a, b):
            return jnp.dot(a, b, preferred_element_type=jnp.float32)

        for copy in copies(step):
            copy.wait()
        value = dot(x_low[...], high_here[step])
        value += dot(x_high[...], low_here[step])
        value += dot(x_high[...], high_here[step])
        squares = value * value * occ_ref[0, :1, :]
        folded = squares[:, :NZ]
        for c in range(1, cols // NZ):
            folded += squares[:, c * NZ : (c + 1) * NZ]
        dens[...] += folded
        for k, out in enumerate(outs):

            @pl.when(step == k)
            def _():
                out[:rows, :] = value

        @pl.when(step == group - 1)
        def _():
            dens_out[...] = jnp.zeros_like(dens_out)
            for line in range(lines):
                sums = jnp.sum(dens[line * NZ : (line + 1) * NZ, :].T, axis=0, keepdims=True) * scale
                dens_out[line : line + 1, :] = sums
            for out in outs:
                for c in range(cols // NZ):
                    out[rows:, c * NZ : (c + 1) * NZ] = dens_out[...]

    weight = pl.BlockSpec(memory_space=pltpu.HBM)
    out = jax.ShapeDtypeStruct((rows + EXTRA, cols), jnp.float32)
    return pl.pallas_call(
        body,
        grid=(group,),
        in_specs=[pl.BlockSpec((count, rows, cols), lambda s: (0, first // rows, 0)), weight, weight, pl.BlockSpec((1, EXTRA, cols), lambda s: (s, 0, 0))],
        out_specs=[pl.BlockSpec((rows + EXTRA, cols), lambda s: (0, 0))] * group + [pl.BlockSpec((EXTRA, NZ), lambda s: (0, 0))],
        out_shape=[out] * group + [jax.ShapeDtypeStruct((EXTRA, NZ), jnp.float32)],
        scratch_shapes=[
            pltpu.VMEM((rows, depth), jnp.bfloat16),
            pltpu.VMEM((rows, depth), jnp.bfloat16),
            pltpu.VMEM((rows, NZ), jnp.float32),
            pltpu.VMEM((group, depth, cols), jnp.bfloat16),
            pltpu.VMEM((group, depth, cols), jnp.bfloat16),
            pltpu.SemaphoreType.DMA((2, group)),
        ],
        compiler_params=pltpu.CompilerParams(vmem_limit_bytes=MOST),
        cost_estimate=pl.CostEstimate(flops=6 * rows * depth * cols * group, bytes_accessed=4 * depth * cols * group + 8 * rows * depth, transcendentals=0),
        name="turn",
    )(blocks, high, low, occ)


def finish(near, far, where, before, after, v_loc, places, scale):
    cols = before.shape[-1]
    lines = len(where[0])
    count = len(where)
    points = count * NY * NZ
    factor = (3.0 / jnp.pi) ** (1.0 / 3.0)
    width = NZ
    chunks = len(near)

    def body(place, *refs):
        near_refs, far_refs = refs[:chunks], refs[chunks : 2 * chunks]
        before_ref, after_ref, v_ref, rotated, density, hpsi, band = refs[2 * chunks :]

        def tile(p, y):
            r, h = place[y % NY // lines], y % lines
            if p < 0 or p == count:
                return (before_ref if p < 0 else after_ref)[r, h * NZ : (h + 1) * NZ, :]
            chunk, line = where[p][h]
            return near_refs[chunk][r, line * NZ : (line + 1) * NZ, :]

        def density_line(p, y):
            r, (chunk, line) = place[y // lines], where[p][y % lines]
            row = near[chunk].shape[1] - EXTRA + line
            return near_refs[chunk][r, row : row + 1, :] + far_refs[chunk][r, line : line + 1, :]

        total = jnp.zeros((8, width), jnp.float32)
        for p in range(count):
            dens = jnp.concatenate([density_line(p, y) for y in range(NY)], axis=0)
            density[p * NY : (p + 1) * NY, :] = dens
            pot = v_ref[p * NY : (p + 1) * NY, :] - factor * jnp.exp(jnp.log(dens) * (1.0 / 3.0))
            pot = jnp.concatenate([pot, jnp.zeros((NZ - NY, NZ), jnp.float32)], axis=0).T
            for y in range(NY):
                here = tile(p, y)
                beside = tile(p - 1, y) + tile(p + 1, y) + tile(p, y - 1) + tile(p, y + 1)
                beside += pltpu.roll(here, 1, 0) + pltpu.roll(here, NZ - 1, 0)
                value = (pot[:, y : y + 1] + 3.0) * here - 0.5 * beside
                at = slice((p * NY + y) * NZ, (p * NY + y + 1) * NZ)
                rotated[at, :] = here
                hpsi[at, :] = value
                total += jnp.sum((here * value).reshape(NZ // 8, 8, width), axis=0)
        band[...] = jnp.sum(total, axis=0, keepdims=True) * scale

    def column(array):
        shape = array.shape
        return pl.BlockSpec(shape[:-1] + (width,), lambda c, _: (0,) * (len(shape) - 1) + (c,))

    def fixed(array):
        shape = array.shape
        return pl.BlockSpec(shape, lambda c, _: (0,) * len(shape))

    v_lines = v_loc.reshape(count * NY, NZ)
    out_column = pl.BlockSpec((points, width), lambda c, _: (0, c))
    return pl.pallas_call(
        body,
        grid_spec=pltpu.PrefetchScalarGridSpec(
            num_scalar_prefetch=1,
            grid=(cols // width,),
            in_specs=[column(a) for a in near] + [fixed(a) for a in far] + [column(before), column(after), fixed(v_lines)],
            out_specs=[
                out_column,
                pl.BlockSpec((count * NY, NZ), lambda c, _: (0, 0)),
                out_column,
                pl.BlockSpec((1, width), lambda c, _: (0, c)),
            ],
        ),
        out_shape=[
            jax.ShapeDtypeStruct((points, cols), jnp.float32),
            jax.ShapeDtypeStruct((count * NY, NZ), jnp.float32),
            jax.ShapeDtypeStruct((points, cols), jnp.float32),
            jax.ShapeDtypeStruct((1, cols), jnp.float32),
        ],
        compiler_params=pltpu.CompilerParams(vmem_limit_bytes=MOST),
        name="finish",
    )(places, *near, *far, before, after, v_lines)


def shards(psi, rot, occ, v_loc):
    points, cols = psi.shape
    depth = rot.shape[0]
    n = lax.axis_size("orb")
    doms = lax.axis_size("dom")
    group = n // 2
    me = lax.axis_index("orb")
    pos = lax.rem(me, group)
    dom = lax.axis_index("dom")
    plane_points = NY * NZ
    planes = points // plane_points
    shares = jnp.stack([pos ^ s for s in range(group)]).astype(jnp.int32)

    def swap(block, s):
        return send(block, "orb", n, lambda a: a ^ s)

    def across(block):
        return send(block, "dom", doms, lambda a: (a + doms // 2) % doms)

    def beside(block):
        return send(block, "dom", doms, lambda a: a ^ 1)

    rows = depth // 4
    quarter = 2 * (dom // (doms // 2)) + lax.rem(dom, 2)
    own = lax.dynamic_slice_in_dim(rot, quarter * rows, rows)
    own = jnp.concatenate([own, jnp.broadcast_to(occ[None, :], (EXTRA, cols))], axis=0)
    firsts = [own[None], collect([swap(own, s) for s in range(1, group)], MARK)]
    places = jnp.stack([quarter, quarter ^ 2, quarter ^ 1, quarter ^ 3]).astype(jnp.int32)
    seconds = [across(first) for first in firsts]
    thirds = [beside(first) for first in firsts]
    fourths = [beside(second) for second in seconds]
    high, low, occ_rows = split_rot(list(zip(firsts, seconds, thirds, fourths)), places)

    lines = NY // group
    lots = [[(0, 0, lines), (planes - 1, 0, lines)], [(p, 0, lines) for p in range(1, planes - 1)]]
    where = [[None] * lines for _ in range(planes)]
    near, far, edges = [], [], []
    gate = []
    for lot in lots:
        height = sum(count for _, _, count in lot) * NZ
        rows = load(psi, [((p * NY + h) // count, count * NZ, lines // count) for p, h, count in lot], group)
        rows = after(rows.reshape(n * height, cols), gate)
        rows = lax.all_to_all(rows, "orb", split_axis=0, concat_axis=0, tiled=True).reshape(n, height, cols)
        at = 0
        for p, h, count in lot:
            for k in range(count):
                where[p][h + k] = (len(near), k)
            *outs, _ = turn(rows, at, count * NZ, high, low, occ_rows, 1.0 / depth)
            at += count * NZ
            if not near:
                gate = [rows, high]
            near.append(jnp.stack([outs[0]] + [swap(outs[s], s) for s in range(1, group)]))
            far.append(swap(near[-1][:, -EXTRA:, :NZ], group))
            if p == 0:
                edges.append(send(near[-1], "dom", doms, lambda a: (a - 1) % doms))
            if p == planes - 1:
                edges.insert(0, send(near[-1], "dom", doms, lambda a: (a + 1) % doms))

    rotated, density, hpsi, band = finish(
        near, far, where, *edges, v_loc, shares, 1.0 / (points * doms)
    )
    return rotated, density.reshape(points), hpsi, lax.psum(band.reshape(cols), "dom")


def solution(mesh):
    placed = (P("dom", "orb"), P(None, "orb"), P("orb"), P("dom"))
    return jax.shard_map(
        shards,
        mesh=mesh,
        in_specs=placed,
        out_specs=(P("dom", "orb"), P("dom"), P("dom", "orb"), P("orb")),
        check_vma=False,
    )
```

```python
import jax
import jax.numpy as jnp
from jax import lax
from jax.experimental import pallas as pl
from jax.experimental.pallas import tpu as pltpu
from jax.sharding import PartitionSpec as P

NY = 8
NZ = 128
EXTRA = 8
VMEM = 32 << 20
MOST = 60 << 20
MARK = 40


def send(block, axis, size, step):
    return lax.ppermute(block, axis, [(a, step(a)) for a in range(size)])


def halves(x):
    high = x.astype(jnp.bfloat16)
    return high, (x - high.astype(jnp.float32)).astype(jnp.bfloat16)


def after(array, others):
    return lax.optimization_barrier((array, *others))[0] if others else array


def load(psi, parts, group):
    cols = psi.shape[1]
    heights = [rows for _, rows, _ in parts]
    total = sum(heights)

    def body(*refs):
        at = 0
        for ref, height in zip(refs, heights):
            for twice in range(2):
                refs[-1][twice, 0, at : at + height, :] = ref[...]
            at += height

    def part(first, rows, step):
        return pl.BlockSpec((rows, cols), lambda s: (first + s * step, 0))

    return pl.pallas_call(
        body,
        grid=(group,),
        in_specs=[part(*p) for p in parts],
        out_specs=pl.BlockSpec((2, 1, total, cols), lambda s: (0, s, 0, 0)),
        out_shape=jax.ShapeDtypeStruct((2, group, total, cols), psi.dtype),
        compiler_params=pltpu.CompilerParams(vmem_limit_bytes=VMEM),
        name="load",
    )(*[psi] * len(parts))


def collect(pieces, span):
    rows, cols = pieces[0].shape
    count = len(pieces)

    def body(*refs):
        for k in range(count):

            @pl.when(pl.program_id(0) == k)
            def _():
                refs[-1][0] = refs[k][...]

    return pl.pallas_call(
        body,
        grid=(count,),
        in_specs=[pl.BlockSpec((rows, cols), lambda s: (0, 0))] * count,
        out_specs=pl.BlockSpec((1, rows, cols), lambda s: (s, 0, 0)),
        out_shape=jax.ShapeDtypeStruct((count, rows, cols), pieces[0].dtype),
        cost_estimate=pl.CostEstimate(flops=span * 10**9, bytes_accessed=8 * count * rows * cols, transcendentals=0),
        name="collect",
    )(*pieces)


def split_rot(sets, places):
    _, rows, cols = sets[0][0].shape
    rows -= EXTRA
    parts = len(sets[0])
    depth = rows * parts
    sizes = [pieces[0].shape[0] for pieces in sets]
    starts = [sum(sizes[:number]) for number in range(len(sets))]
    group = sum(sizes)

    def body(place, *refs):
        ins, (high, low, occ) = refs[: parts * len(sets)], refs[parts * len(sets) :]
        step = pl.program_id(0)
        for number, (start, size) in enumerate(zip(starts, sizes)):

            @pl.when((step >= start) & (step < start + size))
            def _():
                for k in range(parts):
                    piece = ins[number * parts + k]
                    at = pl.ds(pl.multiple_of(place[k] * rows, rows), rows)
                    high[0, at, :], low[0, at, :] = halves(piece[0, :rows, :])
                occ[0] = ins[number * parts][0, rows:, :]

    def block(number):
        return pl.BlockSpec((1, rows + EXTRA, cols), lambda s, _: (jnp.clip(s - starts[number], 0, sizes[number] - 1), 0, 0))

    def out(height):
        return pl.BlockSpec((1, height, cols), lambda s, _: (s, 0, 0))

    return pl.pallas_call(
        body,
        grid_spec=pltpu.PrefetchScalarGridSpec(
            num_scalar_prefetch=1,
            grid=(group,),
            in_specs=[block(number) for number, pieces in enumerate(sets) for _ in pieces],
            out_specs=[out(depth), out(depth), out(EXTRA)],
        ),
        out_shape=[
            jax.ShapeDtypeStruct((group, depth, cols), jnp.bfloat16),
            jax.ShapeDtypeStruct((group, depth, cols), jnp.bfloat16),
            jax.ShapeDtypeStruct((group, EXTRA, cols), jnp.float32),
        ],
        compiler_params=pltpu.CompilerParams(vmem_limit_bytes=VMEM),
        name="split_rot",
    )(places, *[piece for pieces in sets for piece in pieces])


def turn(blocks, first, rows, high, low, occ, scale):
    count, _, cols = blocks.shape
    group, depth, _ = high.shape
    lines = rows // NZ

    def body(x_ref, high_ref, low_ref, occ_ref, *refs):
        outs = refs[:group]
        dens_out, x_high, x_low, dens, high_here, low_here, sems = refs[group:]
        step = pl.program_id(0)

        def copies(s):
            return (
                pltpu.make_async_copy(high_ref.at[s], high_here.at[s], sems.at[0, s]),
                pltpu.make_async_copy(low_ref.at[s], low_here.at[s], sems.at[1, s]),
            )

        @pl.when(step == 0)
        def _():
            for s in range(group):
                for copy in copies(s):
                    copy.start()
            for k in range(count):
                at = slice(k * cols, (k + 1) * cols)
                x_high[:, at], x_low[:, at] = halves(x_ref[k])
            dens[...] = jnp.zeros_like(dens)

        def dot(a, b):
            return jnp.dot(a, b, preferred_element_type=jnp.float32)

        for copy in copies(step):
            copy.wait()
        value = dot(x_low[...], high_here[step])
        value += dot(x_high[...], low_here[step])
        value += dot(x_high[...], high_here[step])
        squares = value * value * occ_ref[0, :1, :]
        folded = squares[:, :NZ]
        for c in range(1, cols // NZ):
            folded += squares[:, c * NZ : (c + 1) * NZ]
        dens[...] += folded
        for k, out in enumerate(outs):

            @pl.when(step == k)
            def _():
                out[:rows, :] = value

        @pl.when(step == group - 1)
        def _():
            dens_out[...] = jnp.zeros_like(dens_out)
            for line in range(lines):
                sums = jnp.sum(dens[line * NZ : (line + 1) * NZ, :].T, axis=0, keepdims=True) * scale
                dens_out[line : line + 1, :] = sums
            for out in outs:
                for c in range(cols // NZ):
                    out[rows:, c * NZ : (c + 1) * NZ] = dens_out[...]

    weight = pl.BlockSpec(memory_space=pltpu.HBM)
    out = jax.ShapeDtypeStruct((rows + EXTRA, cols), jnp.float32)
    return pl.pallas_call(
        body,
        grid=(group,),
        in_specs=[pl.BlockSpec((count, rows, cols), lambda s: (0, first // rows, 0)), weight, weight, pl.BlockSpec((1, EXTRA, cols), lambda s: (s, 0, 0))],
        out_specs=[pl.BlockSpec((rows + EXTRA, cols), lambda s: (0, 0))] * group + [pl.BlockSpec((EXTRA, NZ), lambda s: (0, 0))],
        out_shape=[out] * group + [jax.ShapeDtypeStruct((EXTRA, NZ), jnp.float32)],
        scratch_shapes=[
            pltpu.VMEM((rows, depth), jnp.bfloat16),
            pltpu.VMEM((rows, depth), jnp.bfloat16),
            pltpu.VMEM((rows, NZ), jnp.float32),
            pltpu.VMEM((group, depth, cols), jnp.bfloat16),
            pltpu.VMEM((group, depth, cols), jnp.bfloat16),
            pltpu.SemaphoreType.DMA((2, group)),
        ],
        compiler_params=pltpu.CompilerParams(vmem_limit_bytes=MOST),
        cost_estimate=pl.CostEstimate(flops=6 * rows * depth * cols * group, bytes_accessed=4 * depth * cols * group + 8 * rows * depth, transcendentals=0),
        name="turn",
    )(blocks, high, low, occ)


def finish(near, far, where, before, after, v_loc, places, scale):
    cols = before.shape[-1]
    lines = len(where[0])
    count = len(where)
    points = count * NY * NZ
    factor = (3.0 / jnp.pi) ** (1.0 / 3.0)
    width = NZ
    chunks = len(near)

    def body(place, *refs):
        near_refs, far_refs = refs[:chunks], refs[chunks : 2 * chunks]
        before_ref, after_ref, v_ref, rotated, density, hpsi, band = refs[2 * chunks :]

        def tile(p, y):
            r, h = place[y % NY // lines], y % lines
            if p < 0 or p == count:
                return (before_ref if p < 0 else after_ref)[r, h * NZ : (h + 1) * NZ, :]
            chunk, line = where[p][h]
            return near_refs[chunk][r, line * NZ : (line + 1) * NZ, :]

        def density_line(p, y):
            r, (chunk, line) = place[y // lines], where[p][y % lines]
            row = near[chunk].shape[1] - EXTRA + line
            return near_refs[chunk][r, row : row + 1, :] + far_refs[chunk][r, line : line + 1, :]

        total = jnp.zeros((8, width), jnp.float32)
        for p in range(count):
            dens = jnp.concatenate([density_line(p, y) for y in range(NY)], axis=0)
            density[p * NY : (p + 1) * NY, :] = dens
            pot = v_ref[p * NY : (p + 1) * NY, :] - factor * jnp.exp(jnp.log(dens) * (1.0 / 3.0))
            pot = jnp.concatenate([pot, jnp.zeros((NZ - NY, NZ), jnp.float32)], axis=0).T
            for y in range(NY):
                here = tile(p, y)
                beside = tile(p - 1, y) + tile(p + 1, y) + tile(p, y - 1) + tile(p, y + 1)
                beside += pltpu.roll(here, 1, 0) + pltpu.roll(here, NZ - 1, 0)
                value = (pot[:, y : y + 1] + 3.0) * here - 0.5 * beside
                at = slice((p * NY + y) * NZ, (p * NY + y + 1) * NZ)
                rotated[at, :] = here
                hpsi[at, :] = value
                total += jnp.sum((here * value).reshape(NZ // 8, 8, width), axis=0)
        band[...] = jnp.sum(total, axis=0, keepdims=True) * scale

    def column(array):
        shape = array.shape
        return pl.BlockSpec(shape[:-1] + (width,), lambda c, _: (0,) * (len(shape) - 1) + (c,))

    def fixed(array):
        shape = array.shape
        return pl.BlockSpec(shape, lambda c, _: (0,) * len(shape))

    v_lines = v_loc.reshape(count * NY, NZ)
    out_column = pl.BlockSpec((points, width), lambda c, _: (0, c))
    return pl.pallas_call(
        body,
        grid_spec=pltpu.PrefetchScalarGridSpec(
            num_scalar_prefetch=1,
            grid=(cols // width,),
            in_specs=[column(a) for a in near] + [fixed(a) for a in far] + [column(before), column(after), fixed(v_lines)],
            out_specs=[
                out_column,
                pl.BlockSpec((count * NY, NZ), lambda c, _: (0, 0)),
                out_column,
                pl.BlockSpec((1, width), lambda c, _: (0, c)),
            ],
        ),
        out_shape=[
            jax.ShapeDtypeStruct((points, cols), jnp.float32),
            jax.ShapeDtypeStruct((count * NY, NZ), jnp.float32),
            jax.ShapeDtypeStruct((points, cols), jnp.float32),
            jax.ShapeDtypeStruct((1, cols), jnp.float32),
        ],
        compiler_params=pltpu.CompilerParams(vmem_limit_bytes=MOST),
        name="finish",
    )(places, *near, *far, before, after, v_lines)


def shards(psi, rot, occ, v_loc):
    points, cols = psi.shape
    depth = rot.shape[0]
    n = lax.axis_size("orb")
    doms = lax.axis_size("dom")
    group = n // 2
    me = lax.axis_index("orb")
    pos = lax.rem(me, group)
    dom = lax.axis_index("dom")
    plane_points = NY * NZ
    planes = points // plane_points
    shares = jnp.stack([pos ^ s for s in range(group)]).astype(jnp.int32)

    def swap(block, s):
        return send(block, "orb", n, lambda a: a ^ s)

    def across(block):
        return send(block, "dom", doms, lambda a: (a + doms // 2) % doms)

    def beside(block):
        return send(block, "dom", doms, lambda a: a ^ 1)

    rows = depth // 4
    quarter = 2 * (dom // (doms // 2)) + lax.rem(dom, 2)
    own = lax.dynamic_slice_in_dim(rot, quarter * rows, rows)
    own = jnp.concatenate([own, jnp.broadcast_to(occ[None, :], (EXTRA, cols))], axis=0)
    firsts = [own[None], collect([swap(own, s) for s in range(1, group)], MARK)]
    places = jnp.stack([quarter, quarter ^ 2, quarter ^ 1, quarter ^ 3]).astype(jnp.int32)
    seconds = [across(first) for first in firsts]
    thirds = [beside(first) for first in firsts]
    fourths = [beside(second) for second in seconds]
    high, low, occ_rows = split_rot(list(zip(firsts, seconds, thirds, fourths)), places)

    lines = NY // group
    lots = [[(0, 0, lines), (planes - 1, 0, lines)], [(p, 0, lines) for p in range(1, planes - 1)]]
    where = [[None] * lines for _ in range(planes)]
    near, far = [], []
    gate = []
    for lot in lots:
        height = sum(count for _, _, count in lot) * NZ
        rows = load(psi, [((p * NY + h) // count, count * NZ, lines // count) for p, h, count in lot], group)
        rows = after(rows.reshape(n * height, cols), gate)
        rows = lax.all_to_all(rows, "orb", split_axis=0, concat_axis=0, tiled=True).reshape(n, height, cols)
        at = 0
        for p, h, count in lot:
            for k in range(count):
                where[p][h + k] = (len(near), k)
            *outs, _ = turn(rows, at, count * NZ, high, low, occ_rows, 1.0 / depth)
            at += count * NZ
            if not near:
                gate = [rows, high]
            back = [outs[0]] + [swap(outs[s], s) for s in range(1, group)]
            if not near:
                waiting, near, far = back, [None], [None]
                continue
            near.append(jnp.stack(back))
            far.append(swap(near[-1][:, -EXTRA:, :NZ], group))
            if p == planes - 1:
                before = send(near[-1], "dom", doms, lambda a: (a + 1) % doms)
    near[0] = jnp.stack([waiting[0]] + [after(block, [outs[0]]) for block in waiting[1:]])
    far[0] = swap(near[0][:, -EXTRA:, :NZ], group)
    edges = [before, send(near[0], "dom", doms, lambda a: (a - 1) % doms)]

    rotated, density, hpsi, band = finish(
        near, far, where, *edges, v_loc, shares, 1.0 / (points * doms)
    )
    return rotated, density.reshape(points), hpsi, lax.psum(band.reshape(cols), "dom")


def solution(mesh):
    placed = (P("dom", "orb"), P(None, "orb"), P("orb"), P("dom"))
    return jax.shard_map(
        shards,
        mesh=mesh,
        in_specs=placed,
        out_specs=(P("dom", "orb"), P("dom"), P("dom", "orb"), P("orb")),
        check_vma=False,
    )
```

```python
import jax
import jax.numpy as jnp
from jax import lax
from jax.experimental import pallas as pl
from jax.experimental.pallas import tpu as pltpu
from jax.sharding import PartitionSpec as P

NY = 8
NZ = 128
EXTRA = 8
VMEM = 32 << 20
MOST = 60 << 20
MARK = 40


def send(block, axis, size, step):
    return lax.ppermute(block, axis, [(a, step(a)) for a in range(size)])


def halves(x):
    high = x.astype(jnp.bfloat16)
    return high, (x - high.astype(jnp.float32)).astype(jnp.bfloat16)


def after(array, others):
    return lax.optimization_barrier((array, *others))[0] if others else array


def load(psi, parts, group):
    cols = psi.shape[1]
    heights = [rows for _, rows, _ in parts]
    total = sum(heights)

    def body(*refs):
        at = 0
        for ref, height in zip(refs, heights):
            for twice in range(2):
                refs[-1][twice, 0, at : at + height, :] = ref[...]
            at += height

    def part(first, rows, step):
        return pl.BlockSpec((rows, cols), lambda s: (first + s * step, 0))

    return pl.pallas_call(
        body,
        grid=(group,),
        in_specs=[part(*p) for p in parts],
        out_specs=pl.BlockSpec((2, 1, total, cols), lambda s: (0, s, 0, 0)),
        out_shape=jax.ShapeDtypeStruct((2, group, total, cols), psi.dtype),
        compiler_params=pltpu.CompilerParams(vmem_limit_bytes=VMEM),
        name="load",
    )(*[psi] * len(parts))


def collect(pieces, span):
    rows, cols = pieces[0].shape
    count = len(pieces)

    def body(*refs):
        for k in range(count):

            @pl.when(pl.program_id(0) == k)
            def _():
                refs[-1][0] = refs[k][...]

    return pl.pallas_call(
        body,
        grid=(count,),
        in_specs=[pl.BlockSpec((rows, cols), lambda s: (0, 0))] * count,
        out_specs=pl.BlockSpec((1, rows, cols), lambda s: (s, 0, 0)),
        out_shape=jax.ShapeDtypeStruct((count, rows, cols), pieces[0].dtype),
        cost_estimate=pl.CostEstimate(flops=span * 10**9, bytes_accessed=8 * count * rows * cols, transcendentals=0),
        name="collect",
    )(*pieces)


def split_rot(sets, places):
    _, rows, cols = sets[0][0].shape
    rows -= EXTRA
    parts = len(sets[0])
    depth = rows * parts
    sizes = [pieces[0].shape[0] for pieces in sets]
    starts = [sum(sizes[:number]) for number in range(len(sets))]
    group = sum(sizes)

    def body(place, *refs):
        ins, (high, low, occ) = refs[: parts * len(sets)], refs[parts * len(sets) :]
        step = pl.program_id(0)
        for number, (start, size) in enumerate(zip(starts, sizes)):

            @pl.when((step >= start) & (step < start + size))
            def _():
                for k in range(parts):
                    piece = ins[number * parts + k]
                    at = pl.ds(pl.multiple_of(place[k] * rows, rows), rows)
                    high[0, at, :], low[0, at, :] = halves(piece[0, :rows, :])
                occ[0] = ins[number * parts][0, rows:, :]

    def block(number):
        return pl.BlockSpec((1, rows + EXTRA, cols), lambda s, _: (jnp.clip(s - starts[number], 0, sizes[number] - 1), 0, 0))

    def out(height):
        return pl.BlockSpec((1, height, cols), lambda s, _: (s, 0, 0))

    return pl.pallas_call(
        body,
        grid_spec=pltpu.PrefetchScalarGridSpec(
            num_scalar_prefetch=1,
            grid=(group,),
            in_specs=[block(number) for number, pieces in enumerate(sets) for _ in pieces],
            out_specs=[out(depth), out(depth), out(EXTRA)],
        ),
        out_shape=[
            jax.ShapeDtypeStruct((group, depth, cols), jnp.bfloat16),
            jax.ShapeDtypeStruct((group, depth, cols), jnp.bfloat16),
            jax.ShapeDtypeStruct((group, EXTRA, cols), jnp.float32),
        ],
        compiler_params=pltpu.CompilerParams(vmem_limit_bytes=VMEM),
        name="split_rot",
    )(places, *[piece for pieces in sets for piece in pieces])


def turn(blocks, first, rows, high, low, occ, scale):
    count, _, cols = blocks.shape
    group, depth, _ = high.shape
    lines = rows // NZ

    def body(x_ref, high_ref, low_ref, occ_ref, *refs):
        outs = refs[:group]
        dens_out, x_high, x_low, dens, high_here, low_here, sems = refs[group:]
        step = pl.program_id(0)

        def copies(s):
            return (
                pltpu.make_async_copy(high_ref.at[s], high_here.at[s], sems.at[0, s]),
                pltpu.make_async_copy(low_ref.at[s], low_here.at[s], sems.at[1, s]),
            )

        @pl.when(step == 0)
        def _():
            for s in range(group):
                for copy in copies(s):
                    copy.start()
            for k in range(count):
                at = slice(k * cols, (k + 1) * cols)
                x_high[:, at], x_low[:, at] = halves(x_ref[k])
            dens[...] = jnp.zeros_like(dens)

        def dot(a, b):
            return jnp.dot(a, b, preferred_element_type=jnp.float32)

        for copy in copies(step):
            copy.wait()
        value = dot(x_low[...], high_here[step])
        value += dot(x_high[...], low_here[step])
        value += dot(x_high[...], high_here[step])
        squares = value * value * occ_ref[0, :1, :]
        folded = squares[:, :NZ]
        for c in range(1, cols // NZ):
            folded += squares[:, c * NZ : (c + 1) * NZ]
        dens[...] += folded
        for k, out in enumerate(outs):

            @pl.when(step == k)
            def _():
                out[:rows, :] = value

        @pl.when(step == group - 1)
        def _():
            dens_out[...] = jnp.zeros_like(dens_out)
            for line in range(lines):
                sums = jnp.sum(dens[line * NZ : (line + 1) * NZ, :].T, axis=0, keepdims=True) * scale
                dens_out[line : line + 1, :] = sums
            for out in outs:
                for c in range(cols // NZ):
                    out[rows:, c * NZ : (c + 1) * NZ] = dens_out[...]

    weight = pl.BlockSpec(memory_space=pltpu.HBM)
    out = jax.ShapeDtypeStruct((rows + EXTRA, cols), jnp.float32)
    return pl.pallas_call(
        body,
        grid=(group,),
        in_specs=[pl.BlockSpec((count, rows, cols), lambda s: (0, first // rows, 0)), weight, weight, pl.BlockSpec((1, EXTRA, cols), lambda s: (s, 0, 0))],
        out_specs=[pl.BlockSpec((rows + EXTRA, cols), lambda s: (0, 0))] * group + [pl.BlockSpec((EXTRA, NZ), lambda s: (0, 0))],
        out_shape=[out] * group + [jax.ShapeDtypeStruct((EXTRA, NZ), jnp.float32)],
        scratch_shapes=[
            pltpu.VMEM((rows, depth), jnp.bfloat16),
            pltpu.VMEM((rows, depth), jnp.bfloat16),
            pltpu.VMEM((rows, NZ), jnp.float32),
            pltpu.VMEM((group, depth, cols), jnp.bfloat16),
            pltpu.VMEM((group, depth, cols), jnp.bfloat16),
            pltpu.SemaphoreType.DMA((2, group)),
        ],
        compiler_params=pltpu.CompilerParams(vmem_limit_bytes=MOST),
        cost_estimate=pl.CostEstimate(flops=6 * rows * depth * cols * group, bytes_accessed=4 * depth * cols * group + 8 * rows * depth, transcendentals=0),
        name="turn",
    )(blocks, high, low, occ)


def finish(near, far, where, before, after, v_loc, places, scale):
    cols = before.shape[-1]
    lines = len(where[0])
    count = len(where)
    points = count * NY * NZ
    factor = (3.0 / jnp.pi) ** (1.0 / 3.0)
    width = NZ
    chunks = len(near)

    def body(place, *refs):
        near_refs, far_refs = refs[:chunks], refs[chunks : 2 * chunks]
        before_ref, after_ref, v_ref, rotated, density, hpsi, band = refs[2 * chunks :]

        def tile(p, y):
            r, h = place[y % NY // lines], y % lines
            if p < 0 or p == count:
                return (before_ref if p < 0 else after_ref)[r, h * NZ : (h + 1) * NZ, :]
            chunk, line = where[p][h]
            return near_refs[chunk][r, line * NZ : (line + 1) * NZ, :]

        def density_line(p, y):
            r, (chunk, line) = place[y // lines], where[p][y % lines]
            row = near[chunk].shape[1] - EXTRA + line
            return near_refs[chunk][r, row : row + 1, :] + far_refs[chunk][r, line : line + 1, :]

        total = jnp.zeros((8, width), jnp.float32)
        for p in range(count):
            dens = jnp.concatenate([density_line(p, y) for y in range(NY)], axis=0)
            density[p * NY : (p + 1) * NY, :] = dens
            pot = v_ref[p * NY : (p + 1) * NY, :] - factor * jnp.exp(jnp.log(dens) * (1.0 / 3.0))
            pot = jnp.concatenate([pot, jnp.zeros((NZ - NY, NZ), jnp.float32)], axis=0).T
            for y in range(NY):
                here = tile(p, y)
                beside = tile(p - 1, y) + tile(p + 1, y) + tile(p, y - 1) + tile(p, y + 1)
                beside += pltpu.roll(here, 1, 0) + pltpu.roll(here, NZ - 1, 0)
                value = (pot[:, y : y + 1] + 3.0) * here - 0.5 * beside
                at = slice((p * NY + y) * NZ, (p * NY + y + 1) * NZ)
                rotated[at, :] = here
                hpsi[at, :] = value
                total += jnp.sum((here * value).reshape(NZ // 8, 8, width), axis=0)
        band[...] = jnp.sum(total, axis=0, keepdims=True) * scale

    def column(array):
        shape = array.shape
        return pl.BlockSpec(shape[:-1] + (width,), lambda c, _: (0,) * (len(shape) - 1) + (c,))

    def fixed(array):
        shape = array.shape
        return pl.BlockSpec(shape, lambda c, _: (0,) * len(shape))

    v_lines = v_loc.reshape(count * NY, NZ)
    out_column = pl.BlockSpec((points, width), lambda c, _: (0, c))
    return pl.pallas_call(
        body,
        grid_spec=pltpu.PrefetchScalarGridSpec(
            num_scalar_prefetch=1,
            grid=(cols // width,),
            in_specs=[column(a) for a in near] + [fixed(a) for a in far] + [column(before), column(after), fixed(v_lines)],
            out_specs=[
                out_column,
                pl.BlockSpec((count * NY, NZ), lambda c, _: (0, 0)),
                out_column,
                pl.BlockSpec((1, width), lambda c, _: (0, c)),
            ],
        ),
        out_shape=[
            jax.ShapeDtypeStruct((points, cols), jnp.float32),
            jax.ShapeDtypeStruct((count * NY, NZ), jnp.float32),
            jax.ShapeDtypeStruct((points, cols), jnp.float32),
            jax.ShapeDtypeStruct((1, cols), jnp.float32),
        ],
        compiler_params=pltpu.CompilerParams(vmem_limit_bytes=MOST),
        name="finish",
    )(places, *near, *far, before, after, v_lines)


def shards(psi, rot, occ, v_loc):
    points, cols = psi.shape
    depth = rot.shape[0]
    n = lax.axis_size("orb")
    doms = lax.axis_size("dom")
    group = n // 2
    me = lax.axis_index("orb")
    pos = lax.rem(me, group)
    dom = lax.axis_index("dom")
    plane_points = NY * NZ
    planes = points // plane_points
    shares = jnp.stack([pos ^ s for s in range(group)]).astype(jnp.int32)

    def swap(block, s):
        return send(block, "orb", n, lambda a: a ^ s)

    def across(block):
        return send(block, "dom", doms, lambda a: (a + doms // 2) % doms)

    def beside(block):
        return send(block, "dom", doms, lambda a: a ^ 1)

    rows = depth // 4
    quarter = 2 * (dom // (doms // 2)) + lax.rem(dom, 2)
    own = lax.dynamic_slice_in_dim(rot, quarter * rows, rows)
    own = jnp.concatenate([own, jnp.broadcast_to(occ[None, :], (EXTRA, cols))], axis=0)
    firsts = [own[None], collect([swap(own, s) for s in range(1, group)], MARK)]
    places = jnp.stack([quarter, quarter ^ 2, quarter ^ 1, quarter ^ 3]).astype(jnp.int32)
    seconds = [across(first) for first in firsts]
    thirds = [beside(first) for first in firsts]
    fourths = [beside(second) for second in seconds]
    high, low, occ_rows = split_rot(list(zip(firsts, seconds, thirds, fourths)), places)

    lines = NY // group
    lots = [[(0, 0, lines), (planes - 1, 0, lines)], [(p, 0, lines) for p in range(1, planes - 1)]]
    where = [[None] * lines for _ in range(planes)]
    near, far = [], []
    gate = []
    for lot in lots:
        height = sum(count for _, _, count in lot) * NZ
        rows = load(psi, [((p * NY + h) // count, count * NZ, lines // count) for p, h, count in lot], group)
        rows = after(rows.reshape(n * height, cols), gate)
        rows = lax.all_to_all(rows, "orb", split_axis=0, concat_axis=0, tiled=True).reshape(n, height, cols)
        at = 0
        for p, h, count in lot:
            for k in range(count):
                where[p][h + k] = (len(near), k)
            *outs, dens = turn(rows, at, count * NZ, high, low, occ_rows, 1.0 / depth)
            at += count * NZ
            if not near:
                gate = [rows, high]
            back = [outs[0]] + [swap(outs[s], s) for s in range(1, group)]
            if not near:
                waiting, near, far = back, [None], [None]
                continue
            near.append(jnp.stack(back))
            if lot is lots[-1]:
                far.append(jnp.stack([swap(dens, group + s) for s in range(group)]))
            else:
                far.append(swap(near[-1][:, -EXTRA:, :NZ], group))
            if p == planes - 1:
                before = send(near[-1], "dom", doms, lambda a: (a + 1) % doms)
    near[0] = jnp.stack([waiting[0]] + [after(block, [outs[0]]) for block in waiting[1:]])
    far[0] = swap(near[0][:, -EXTRA:, :NZ], group)
    edges = [before, send(near[0], "dom", doms, lambda a: (a - 1) % doms)]

    rotated, density, hpsi, band = finish(
        near, far, where, *edges, v_loc, shares, 1.0 / (points * doms)
    )
    return rotated, density.reshape(points), hpsi, lax.psum(band.reshape(cols), "dom")


def solution(mesh):
    placed = (P("dom", "orb"), P(None, "orb"), P("orb"), P("dom"))
    return jax.shard_map(
        shards,
        mesh=mesh,
        in_specs=placed,
        out_specs=(P("dom", "orb"), P("dom"), P("dom", "orb"), P("orb")),
        check_vma=False,
    )
```
